32 devices in a mesh: grp: 2 (over x), date: 16 (over z, y, core).
Axes of the slice: x: 2, y: 2, z: 4, core: 2. Of those that a mesh axis runs over, the one named last changes fastest.
Arguments:
- amplitude: bfloat16 [32, 256, 1024], P('date', 'grp'), parts along dimension 1, may hold values from 0.01 to 600, as said below
- phase: bfloat16 [32, 256, 1024], P('date', 'grp'), parts along dimension 1, may hold values from -3.1416 to 3.1416
- offset_code: int32 [32, 5], P('date'), may hold values from 0 to 4, each once within a row
- look_half: int32 [256, 1024], P('grp'), parts along dimension 0, may hold values from 1 to 3
Outputs:
- filtered: bfloat16 [32, 5, 2, 256, 1024], P('date', None, None, 'grp'), parts along dimension 3
- coherence: bfloat16 [32, 5, 256, 1024], P('date', None, 'grp'), parts along dimension 2
The draws below stay inside these ranges and needn't reach their ends.
There are 2 independent parts, one for each index of `grp`. The reference program is written for one: setup_inputs(seed, part) draws one part's arguments, and reference() takes and returns one part's arrays. A program takes and returns all parts, laid end to end along the dimension named above; an argument that names none is the same for every part. Nothing has to cross between parts.
Inputs may be any that keep to these rules, and one draw needn't show every extreme that they name: `offset_code`: each row holds every value 0 to 4 exactly once. `amplitude`: positive amplitudes.
All inputs are finite; a program needn't handle non-finite values.
Results may differ from the reference program's by a relative error of at most 0.0004.
Values may be sent and summed in bfloat16 or wider, within the bound.
No kernel may reach another device: no remote copies, remote signals or barrier semaphores. Data moves between devices by JAX's collectives and lax.ppermute only.
A program may use at most 128 MiB of HBM per device.

```python
import math
import jax
import jax.numpy as jnp
from jax import lax

ROWS = 128
COLS = 1024
REACH = 5
DATES = 32


def draw_amplitude(key, part):
    key = jax.random.fold_in(key, 11)
    keys = jax.random.split(key, 4)
    position = jnp.arange(DATES, dtype=jnp.float32) / (DATES - 1)
    trend = jnp.exp(position * math.log(10.0)) * jax.random.uniform(keys[0], (DATES,), jnp.float32, 0.7, 1.4)
    base_level = jnp.exp(jax.random.uniform(keys[1], (ROWS, COLS), jnp.float32, math.log(0.5), math.log(2.0)))
    spread = jax.random.uniform(keys[2], (ROWS, COLS), jnp.float32, 0.05, 1.2)
    noise = jnp.clip(jax.random.normal(keys[3], (DATES, ROWS, COLS), jnp.float32), -2.5, 2.5)
    values = trend[:, None, None] * base_level[None] * jnp.exp(spread[None] * noise)
    return values.astype(jnp.bfloat16)


def draw_phase(key, part):
    key = jax.random.fold_in(key, 12)
    keys = jax.random.split(key, 4)
    common = jax.random.uniform(keys[0], (ROWS, COLS), jnp.float32, -math.pi, math.pi)
    motion = jax.random.uniform(keys[1], (ROWS, COLS), jnp.float32, -0.4, 0.4)
    scatter = jax.random.uniform(keys[2], (ROWS, COLS), jnp.float32, 0.05, 1.0)
    noise = jnp.clip(jax.random.normal(keys[3], (DATES, ROWS, COLS), jnp.float32), -4.0, 4.0)
    position = jnp.arange(DATES, dtype=jnp.float32)
    raw_phase = common[None] + motion[None] * position[:, None, None] + scatter[None] * noise
    wrapped = jnp.mod(raw_phase + math.pi, 2.0 * math.pi) - math.pi
    return wrapped.astype(jnp.bfloat16)


def touch_ends(drawn, rng, low, top_value):
    dims = drawn.shape
    place = [jax.random.randint(jax.random.fold_in(rng, axis), (), 0, dims[axis]) for axis in range(len(dims))]
    drawn = drawn.at[tuple(place)].set(low)
    longest = dims.index(max(dims))
    place[longest] = (place[longest] + 1) % dims[longest]
    return drawn.at[tuple(place)].set(top_value)


def setup_inputs(seed: int = 0, part: int = 0) -> dict:
    key_list = jax.random.split(jax.random.key(seed), 5)
    part_splits = jax.random.split(jax.random.fold_in(key_list[4], part), 5)
    amplitude = draw_amplitude(jax.random.fold_in(jax.random.fold_in(key_list[4], part), 71), part)
    phase = draw_phase(jax.random.fold_in(jax.random.fold_in(key_list[4], part), 71), part)
    offset_code = jax.vmap(lambda own: jax.random.permutation(own, REACH))(jax.random.split(key_list[2], DATES)).reshape((DATES, REACH)).astype(jnp.int32)
    look_half = touch_ends(jax.random.randint(part_splits[3], (ROWS, COLS), 1, 4), jax.random.fold_in(part_splits[3], 1), 1, 3).astype(jnp.int32)
    return {"amplitude": amplitude, "phase": phase, "offset_code": offset_code, "look_half": look_half}


disp_gain = 4.0

def shifted(source, offset, along):
    length = source.shape[along]
    widths = [(0, 0)] * source.ndim
    if offset > 0:
        widths[along] = (0, offset)
        begin_at = offset
    else:
        widths[along] = (-offset, 0)
        begin_at = 0
    padded = jnp.pad(source, widths)
    return lax.slice_in_dim(padded, begin_at, begin_at + length, axis=along)

def across(rowsum, radius):
    column_axis = rowsum.ndim - 1
    summed = rowsum
    for reach_now in range(1, radius + 1):
        summed = summed + shifted(rowsum, reach_now, column_axis) + shifted(rowsum, -reach_now, column_axis)
    return summed

def looked(source, look_half):
    row_axis = source.ndim - 2
    rows_one = source + shifted(source, 1, row_axis) + shifted(source, -1, row_axis)
    rows_two = rows_one + shifted(source, 2, row_axis) + shifted(source, -2, row_axis)
    rows_three = rows_two + shifted(source, 3, row_axis) + shifted(source, -3, row_axis)
    box_one = across(rows_one, 1)
    box_two = across(rows_two, 2)
    box_three = across(rows_three, 3)
    return jnp.where(look_half == 1, box_one, jnp.where(look_half == 2, box_two, box_three))

def neighbours(source):
    row_axis = source.ndim - 2
    rows_one = source + shifted(source, 1, row_axis) + shifted(source, -1, row_axis)
    return across(rows_one, 1)

def reference(amplitude, phase, offset_code, look_half):
    magnitude = amplitude.astype(jnp.float32)
    angles = phase.astype(jnp.float32)
    real_part = magnitude * jnp.cos(angles)
    imag_part = magnitude * jnp.sin(angles)
    first_moment = lax.optimization_barrier(jnp.sum(magnitude, axis=0))
    second_moment = lax.optimization_barrier(jnp.sum(magnitude * magnitude, axis=0))
    weight = 1.0 / (1.0 + disp_gain * (DATES * second_moment / (first_moment * first_moment) - 1.0))

    def date_power(parts_pair):
        return looked(weight * (parts_pair[0] * parts_pair[0] + parts_pair[1] * parts_pair[1]), look_half)
    power = lax.map(date_power, (real_part, imag_part))

    def one_date(date_index):
        own_real = lax.dynamic_index_in_dim(real_part, date_index, 0, keepdims=False)
        own_imag = lax.dynamic_index_in_dim(imag_part, date_index, 0, keepdims=False)
        own_power = lax.dynamic_index_in_dim(power, date_index, 0, keepdims=False)
        filter_list = []
        gamma_list = []
        for offset in range(1, REACH + 1):
            partner = jnp.minimum(date_index + offset, DATES - 1).astype(jnp.int32)
            exists_mask = date_index + offset < DATES
            far_real = lax.dynamic_index_in_dim(real_part, partner, 0, keepdims=False)
            far_imag = lax.dynamic_index_in_dim(imag_part, partner, 0, keepdims=False)
            far_power = lax.dynamic_index_in_dim(power, partner, 0, keepdims=False)
            inter_real = own_real * far_real + own_imag * far_imag
            inter_imag = own_imag * far_real - own_real * far_imag
            look_real = looked(weight * inter_real, look_half)
            look_imag = looked(weight * inter_imag, look_half)
            product = jnp.where(exists_mask, own_power * far_power, 1.0)
            scaling = jnp.where(exists_mask, lax.rsqrt(product), 0.0)
            unit_real = look_real * scaling
            unit_imag = look_imag * scaling
            coherent = jnp.sqrt(unit_real * unit_real + unit_imag * unit_imag)
            mean_real = neighbours(unit_real) / 9.0
            mean_imag = neighbours(unit_imag) / 9.0
            out_real = coherent * unit_real + (1.0 - coherent) * mean_real
            out_imag = coherent * unit_imag + (1.0 - coherent) * mean_imag
            filter_list.append(jnp.stack((out_real, out_imag), axis=0))
            gamma_list.append(coherent)
        stacked_filter = jnp.stack(filter_list, axis=0)
        stacked_gamma = jnp.stack(gamma_list, axis=0)
        slot_codes = lax.dynamic_index_in_dim(offset_code, date_index, 0, keepdims=False).astype(jnp.int32)
        return (stacked_filter[slot_codes].astype(jnp.bfloat16), stacked_gamma[slot_codes].astype(jnp.bfloat16))
    filtered, coherence = lax.map(one_date, jnp.arange(DATES, dtype=jnp.int32))
    return (filtered, coherence)
```

```python
import functools

import jax
import jax.numpy as jnp
import numpy as np
from jax import lax
from jax.experimental import pallas as pl
from jax.experimental.pallas import tpu as pltpu
from jax.sharding import PartitionSpec as P

REACH = 5
DISP_GAIN = 4.0
LANES = 128
CHUNK = 16

SIN_TERMS = (1.0, -1.0 / 6, 1.0 / 120, -1.0 / 5040, 1.0 / 362880, -1.0 / 39916800, 1.0 / 6227020800)
COS_TERMS = (1.0, -1.0 / 2, 1.0 / 24, -1.0 / 720, 1.0 / 40320, -1.0 / 3628800, 1.0 / 479001600)


def series(square, terms):
    total = jnp.full_like(square, terms[-1])
    for term in terms[-2::-1]:
        total = total * square + term
    return total


def slc_of(amplitude, phase):
    amplitude = amplitude.astype(jnp.float32)
    half = phase.astype(jnp.float32) * 0.5
    square = half * half
    sine = half * series(square, SIN_TERMS)
    cosine = series(square, COS_TERMS)
    scaled = (amplitude + amplitude) * sine
    return amplitude - scaled * sine, scaled * cosine


def trig_kernel(amp_ref, phase_ref, slc_ref):
    rows = amp_ref.shape[1]

    def step(index, carry):
        here = pl.ds(pl.multiple_of(index * CHUNK, CHUNK), CHUNK)
        real, imag = slc_of(amp_ref[0, here], phase_ref[0, here])
        slc_ref[0, 0, here] = real
        slc_ref[0, 1, here] = imag
        return carry

    lax.fori_loop(0, rows // CHUNK, step, 0)


def slc_tiles(amplitude, phase):
    dates, rows, cols = amplitude.shape
    block = pl.BlockSpec((1, rows, cols), lambda d: (d, 0, 0))
    return pl.pallas_call(
        trig_kernel,
        grid=(dates,),
        in_specs=[block, block],
        out_specs=pl.BlockSpec((1, 2, rows, cols), lambda d: (d, 0, 0, 0)),
        out_shape=jax.ShapeDtypeStruct((dates, 2, rows, cols), jnp.float32),
        cost_estimate=pl.CostEstimate(flops=dates * rows * cols * 40, bytes_accessed=dates * rows * cols * 12, transcendentals=0),
    )(amplitude, phase)


def beside(tiles, step):
    lane = lax.broadcasted_iota(jnp.int32, tiles[0].shape, 1)
    turned = [pltpu.roll(tile, (-step) % LANES, 1) for tile in tiles]
    count = len(tiles)
    out = []
    for c in range(count):
        if step > 0:
            other = turned[c + 1] if c + 1 < count else jnp.zeros_like(tiles[0])
            out.append(jnp.where(lane >= LANES - step, other, turned[c]))
        else:
            other = turned[c - 1] if c > 0 else jnp.zeros_like(tiles[0])
            out.append(jnp.where(lane < -step, other, turned[c]))
    return out


def put_column_sums(tiles, sums_ref, row, rows):
    total = tiles
    for j in (1, 2, 3):
        after = beside(tiles, j)
        before = beside(tiles, -j)
        total = [t + a + b for t, a, b in zip(total, after, before)]
        for c, value in enumerate(total):
            high = value.astype(jnp.bfloat16)
            low = (value - high.astype(jnp.float32)).astype(jnp.bfloat16)
            sums_ref[j - 1, pl.ds(row, CHUNK), c * LANES : (c + 1) * LANES] = high
            sums_ref[j - 1, pl.ds(rows + row, CHUNK), c * LANES : (c + 1) * LANES] = low


def looked(sums_ref, band_ref, half, columns):
    box = [
        jnp.dot(band_ref[h], sums_ref[h, :, columns], preferred_element_type=jnp.float32)
        for h in range(3)
    ]
    return jnp.where(half == 1, box[0], jnp.where(half == 2, box[1], box[2]))


def main_kernel(
    dates_dev, slot_ref, valid_ref, own_ref, far_ref, weight_ref, half_ref, band_ref,
    filtered_ref, gamma_ref, inverse_ref, sums_ref, unit_ref,
):
    rows, cols = weight_ref.shape
    tiles = cols // LANES
    wide = 2 * LANES
    ext = dates_dev + REACH
    step = pl.program_id(0)
    date = step // REACH
    offset = step % REACH + 1

    def tile_of(c):
        return slice(c * LANES, (c + 1) * LANES)

    @pl.when(step == 0)
    def _():
        unit_ref[:, :, 0:8, :] = jnp.zeros((2, tiles, 8, LANES), jnp.float32)
        unit_ref[:, :, rows + 8 : rows + 16, :] = jnp.zeros((2, tiles, 8, LANES), jnp.float32)

        def power_date(d, slc_ref, base):
            for row in range(0, rows, CHUNK):
                here = slice(row, row + CHUNK)
                power = []
                for c in range(tiles):
                    real = slc_ref[d, 0, here, tile_of(c)]
                    imag = slc_ref[d, 1, here, tile_of(c)]
                    power.append(weight_ref[here, tile_of(c)] * (real * real + imag * imag))
                put_column_sums(power, sums_ref.at[0], row, rows)
            valid = valid_ref[base + d] != 0
            for n in range(0, cols, wide):
                columns = slice(n, n + wide)
                power = looked(sums_ref.at[0], band_ref, half_ref[:, columns], columns)
                inverse_ref[base + d, :, columns] = jnp.where(valid, lax.rsqrt(power), 0.0)

        def own_power(d, carry):
            power_date(d, own_ref, 0)
            return carry

        def far_power(d, carry):
            power_date(d, far_ref, dates_dev)
            return carry

        lax.fori_loop(0, dates_dev, own_power, 0)
        lax.fori_loop(0, REACH, far_power, 0)

    far = date + offset

    def pair(other_ref, other):
        for row in range(0, rows, CHUNK):
            here = slice(row, row + CHUNK)
            reals, imags = [], []
            for c in range(tiles):
                weight = weight_ref[here, tile_of(c)]
                real = weight * own_ref[date, 0, here, tile_of(c)]
                imag = weight * own_ref[date, 1, here, tile_of(c)]
                far_real = other_ref[other, 0, here, tile_of(c)]
                far_imag = other_ref[other, 1, here, tile_of(c)]
                reals.append(real * far_real + imag * far_imag)
                imags.append(imag * far_real - real * far_imag)
            put_column_sums(reals, sums_ref.at[0], row, rows)
            put_column_sums(imags, sums_ref.at[1], row, rows)

    @pl.when(far < dates_dev)
    def _():
        pair(own_ref, far)

    @pl.when(far >= dates_dev)
    def _():
        pair(far_ref, far - dates_dev)

    for n in range(0, cols, wide):
        columns = slice(n, n + wide)
        half = half_ref[:, columns]
        scale = inverse_ref[date, :, columns] * inverse_ref[far, :, columns]
        for part in range(2):
            unit = looked(sums_ref.at[part], band_ref, half, columns) * scale
            for k in range(wide // LANES):
                unit_ref[part, n // LANES + k, 8 : rows + 8, :] = unit[:, tile_of(k)]

    for row in range(0, rows, CHUNK):
        units, means = [], []
        for part in range(2):
            centre = [unit_ref[part, c, row + 8 : row + 8 + CHUNK, :] for c in range(tiles)]
            column = [
                centre[c]
                + unit_ref[part, c, row + 7 : row + 7 + CHUNK, :]
                + unit_ref[part, c, row + 9 : row + 9 + CHUNK, :]
                for c in range(tiles)
            ]
            after, before = beside(column, 1), beside(column, -1)
            units.append(centre)
            means.append([(m + a + b) * (1.0 / 9.0) for m, a, b in zip(column, after, before)])
        for c in range(tiles):
            real, imag = units[0][c], units[1][c]
            gamma = jnp.sqrt(real * real + imag * imag)
            for part in range(2):
                mean = means[part][c]
                value = mean + gamma * (units[part][c] - mean)
                filtered_ref[0, 0, part, row : row + CHUNK, tile_of(c)] = value.astype(jnp.bfloat16)
            gamma_ref[0, 0, row : row + CHUNK, tile_of(c)] = gamma.astype(jnp.bfloat16)


def band_of(rows):
    gap = np.abs(np.arange(rows)[:, None] - np.arange(rows)[None, :])
    band = np.stack([(gap <= h).astype(np.float32) for h in (1, 2, 3)])
    return jnp.asarray(np.concatenate([band, band], axis=2), jnp.bfloat16)


def interferograms(own, far, weight, look_half, slot, valid):
    dates_dev, _, rows, cols = own.shape
    ext = dates_dev + REACH
    whole = pl.BlockSpec(memory_space=pltpu.VMEM)
    spec = pltpu.PrefetchScalarGridSpec(
        num_scalar_prefetch=2,
        grid=(dates_dev * REACH,),
        in_specs=[whole] * 5,
        out_specs=[
            pl.BlockSpec((1, 1, 2, rows, cols), lambda s, slot, valid: (s // REACH, slot[s], 0, 0, 0)),
            pl.BlockSpec((1, 1, rows, cols), lambda s, slot, valid: (s // REACH, slot[s], 0, 0)),
        ],
        scratch_shapes=[
            pltpu.VMEM((ext, rows, cols), jnp.float32),
            pltpu.VMEM((2, 3, 2 * rows, cols), jnp.bfloat16),
            pltpu.VMEM((2, cols // LANES, rows + 16, LANES), jnp.float32),
        ],
    )
    return pl.pallas_call(
        functools.partial(main_kernel, dates_dev),
        grid_spec=spec,
        out_shape=[
            jax.ShapeDtypeStruct((dates_dev, REACH, 2, rows, cols), jnp.bfloat16),
            jax.ShapeDtypeStruct((dates_dev, REACH, rows, cols), jnp.bfloat16),
        ],
        compiler_params=pltpu.CompilerParams(vmem_limit_bytes=48 * 2**20),
        cost_estimate=pl.CostEstimate(flops=10**10, bytes_accessed=2 * 10**7, transcendentals=10**6),
    )(slot, valid, own, far, weight, look_half, band_of(rows))


def from_behind(value, axis, steps):
    count = lax.axis_size(axis)
    return lax.ppermute(value, axis, [(source, source + steps) for source in range(max(0, -steps), min(count, count - steps))])


def weight_of(amplitude, total_dates):
    mine = lax.all_to_all(amplitude, "date", 1, 0, tiled=True).astype(jnp.float32)
    first = jnp.sum(mine, axis=0)
    second = jnp.sum(mine * mine, axis=0)
    weight = 1.0 / (1.0 + DISP_GAIN * (total_dates * second / (first * first) - 1.0))
    return lax.all_gather(weight, "date", axis=0, tiled=True)


def local(amplitude, phase, offset_code, look_half):
    dates_dev = amplitude.shape[0]
    total_dates = dates_dev * lax.axis_size("date")
    first_date = lax.axis_index("date") * dates_dev
    pieces = []
    for hop in range(1, (REACH + dates_dev - 1) // dates_dev + 1):
        take = min(dates_dev, REACH - (hop - 1) * dates_dev)
        pieces.append((from_behind(amplitude[:take], "date", -hop), from_behind(phase[:take], "date", -hop)))
    weight = weight_of(amplitude, total_dates)
    own = slc_tiles(amplitude, phase)
    far = slc_tiles(*(jnp.concatenate([piece[k] for piece in pieces]) for k in range(2)))
    valid = (first_date + jnp.arange(dates_dev + REACH) < total_dates).astype(jnp.int32)
    same = offset_code[:, None, :] == jnp.arange(REACH, dtype=jnp.int32)[None, :, None]
    slot = jnp.sum(jnp.where(same, jnp.arange(REACH, dtype=jnp.int32), 0), axis=2, dtype=jnp.int32).reshape(-1)
    filtered, coherence = interferograms(own, far, weight, look_half, slot, valid)
    return filtered, coherence


def solution(mesh):
    return jax.shard_map(
        local,
        mesh=mesh,
        in_specs=(P("date", "grp", None), P("date", "grp", None), P("date", None), P("grp", None)),
        out_specs=(P("date", None, None, "grp", None), P("date", None, "grp", None)),
        check_vma=False,
    )
```

```python
import functools

import jax
import jax.numpy as jnp
import numpy as np
from jax import lax
from jax.experimental import pallas as pl
from jax.experimental.pallas import tpu as pltpu
from jax.sharding import PartitionSpec as P

REACH = 5
DISP_GAIN = 4.0
LANES = 128
CHUNK = 16
PAD = 8

SIN_TERMS = (1.0, -1.0 / 6, 1.0 / 120, -1.0 / 5040, 1.0 / 362880, -1.0 / 39916800, 1.0 / 6227020800)
COS_TERMS = (1.0, -1.0 / 2, 1.0 / 24, -1.0 / 720, 1.0 / 40320, -1.0 / 3628800, 1.0 / 479001600)


def series(square, terms):
    total = jnp.full_like(square, terms[-1])
    for term in terms[-2::-1]:
        total = total * square + term
    return total


def slc_of(amplitude, phase):
    amplitude = amplitude.astype(jnp.float32)
    half = phase.astype(jnp.float32) * 0.5
    square = half * half
    sine = half * series(square, SIN_TERMS)
    cosine = series(square, COS_TERMS)
    scaled = (amplitude + amplitude) * sine
    return amplitude - scaled * sine, scaled * cosine


def over_rows(rows, body):
    def step(index, carry):
        body(pl.ds(pl.multiple_of(index * CHUNK, CHUNK), CHUNK))
        return carry

    lax.fori_loop(0, rows // CHUNK, step, 0)


def cost(pixels, flops, nbytes):
    return pl.CostEstimate(flops=pixels * flops, bytes_accessed=pixels * nbytes, transcendentals=0)


VMEM = pl.BlockSpec(memory_space=pltpu.VMEM)
SMEM = pl.BlockSpec(memory_space=pltpu.SMEM)


def slc_dates(place_ref, sources, slc_ref):
    odd = place_ref[0] != 0

    def body(n, carry):
        columns = pl.ds(pl.multiple_of(n * LANES, LANES), LANES)
        for date, pair, index, other, other_index in sources:
            found = []
            for k in range(2):
                value = pair[k][index, :, columns].astype(jnp.float32)
                if other is not None:
                    value = jnp.where(odd, value, other[k][other_index, :, columns].astype(jnp.float32))
                found.append(value.T)
            slc_ref[date, 0, columns], slc_ref[date, 1, columns] = slc_of(*found)
        return carry

    lax.fori_loop(0, sources[0][1][0].shape[2] // LANES, body, 0)


def first_slc_kernel(place_ref, own_amp, own_phase, next_amp, next_phase, slc_ref):
    own, following = (own_amp, own_phase), (next_amp, next_phase)
    slc_dates(
        place_ref,
        [(0, own, 0, None, 0), (1, own, 1, None, 0), (4, following, 0, None, 0), (5, following, 1, None, 0)],
        slc_ref,
    )


def second_slc_kernel(place_ref, mate_amp, mate_phase, via_amp, via_phase, last_ref, begun_ref, slc_ref):
    mate, via, last = (mate_amp, mate_phase), (via_amp, via_phase), (last_ref.at[0:1], last_ref.at[1:2])
    slc_dates(place_ref, [(2, via, 0, mate, 0), (3, via, 1, mate, 1), (6, last, 0, via, 0)], slc_ref)


def slc_turned(kernel, place, *arrays, begun=None):
    dates, rows, cols = arrays[0].shape
    if begun is not None:
        arrays = arrays + (begun,)
    return pl.pallas_call(
        kernel,
        in_specs=[SMEM] + [VMEM] * len(arrays),
        out_specs=VMEM,
        out_shape=jax.ShapeDtypeStruct((dates + REACH, 2, cols, rows), jnp.float32),
        input_output_aliases={} if begun is None else {len(arrays): 0},
        compiler_params=pltpu.CompilerParams(vmem_limit_bytes=16 * 2**20),
        cost_estimate=cost(dates * rows * cols, 8000, 12),
    )(place, *arrays)


def gate_kernel(*refs):
    pass


def after(values, *others):
    ANY = pl.BlockSpec(memory_space=pl.ANY)
    return pl.pallas_call(
        gate_kernel,
        in_specs=[ANY] * (len(values) + len(others)),
        out_specs=[ANY] * len(values),
        out_shape=[jax.ShapeDtypeStruct(v.shape, v.dtype) for v in values],
        input_output_aliases={k: k for k in range(len(values))},
    )(*values, *others)


def moments_kernel(place_ref, own_ref, mate_ref, phase_ref, pieces_ref, early_ref):
    chips, _, deep, cols = pieces_ref.shape
    half = chips * deep
    start = place_ref[0] * half
    early_ref[0] = own_ref[0]
    early_ref[1] = phase_ref[0]

    for row in range(0, half, CHUNK):
        there = pl.ds(pl.multiple_of(start + row, CHUNK), CHUNK)
        values = [ref[d, there].astype(jnp.float32) for ref in (own_ref, mate_ref) for d in range(ref.shape[0])]
        squares = [v * v for v in values]
        for which, total in enumerate((sum(values[1:], values[0]), sum(squares[1:], squares[0]))):
            for low in range(0, CHUNK, min(deep, CHUNK)):
                chip, inside = (row + low) // deep, (row + low) % deep
                size = min(deep, CHUNK)
                pieces_ref[chip, which, inside : inside + size] = total[low : low + size]


def moment_pieces(place, own, mate, phase, chips):
    _, rows, cols = own.shape
    half = rows // 2
    return pl.pallas_call(
        moments_kernel,
        in_specs=[SMEM, VMEM, VMEM, VMEM],
        out_specs=[VMEM, VMEM],
        out_shape=[
            jax.ShapeDtypeStruct((chips, 2, half // chips, cols), jnp.float32),
            jax.ShapeDtypeStruct((2, rows, cols), jnp.bfloat16),
        ],
        cost_estimate=cost(half * cols, 12, 24),
    )(place, own, mate, phase)


def beside(tiles, step):
    lane = lax.broadcasted_iota(jnp.int32, tiles[0].shape, 1)
    turned = [pltpu.roll(tile, (-step) % LANES, 1) for tile in tiles]
    count = len(tiles)
    out = []
    for c in range(count):
        if step > 0:
            other = turned[c + 1] if c + 1 < count else jnp.zeros_like(tiles[0])
            out.append(jnp.where(lane >= LANES - step, other, turned[c]))
        else:
            other = turned[c - 1] if c > 0 else jnp.zeros_like(tiles[0])
            out.append(jnp.where(lane < -step, other, turned[c]))
    return out


def put_column_sums(field_ref, sums_ref):
    cols, rows = sums_ref.shape[1], sums_ref.shape[2] // 2
    for c in range(0, cols, CHUNK):
        total = field_ref[PAD + c : PAD + c + CHUNK]
        for j in (1, 2, 3):
            total = total + (field_ref[PAD + c + j : PAD + c + j + CHUNK] + field_ref[PAD + c - j : PAD + c - j + CHUNK])
            high = total.astype(jnp.bfloat16)
            sums_ref[j - 1, c : c + CHUNK, :rows] = high
            sums_ref[j - 1, c : c + CHUNK, rows:] = (total - high.astype(jnp.float32)).astype(jnp.bfloat16)


def looked(sums_ref, band_ref, half, columns):
    box = [
        lax.dot_general(band_ref[h], sums_ref[h, columns, :], (((1,), (1,)), ((), ())), preferred_element_type=jnp.float32)
        for h in range(3)
    ]
    return jnp.where(half == 1, box[0], jnp.where(half == 2, box[1], box[2]))


def main_kernel(
    dates_dev, slot_ref, valid_ref, place_ref, slc_ref, mine_ref, other_half_ref, half_ref, band_ref,
    filtered_ref, gamma_ref, flat_ref, weight_ref, inverse_ref, field_ref, sums_ref, unit_ref,
):
    cols, rows = weight_ref.shape
    tiles = cols // LANES
    wide = 2 * LANES
    step = pl.program_id(0)
    date = step // REACH
    far = date + step % REACH + 1

    def tile_of(c):
        return slice(c * LANES, (c + 1) * LANES)

    @pl.when(step == 0)
    def _():
        unit_ref[:, :, 0:PAD, :] = jnp.zeros((2, tiles, PAD, LANES), jnp.float32)
        unit_ref[:, :, rows + PAD : rows + 2 * PAD, :] = jnp.zeros((2, tiles, PAD, LANES), jnp.float32)
        field_ref[:, 0:PAD, :] = jnp.zeros((2, PAD, rows), jnp.float32)
        field_ref[:, cols + PAD : cols + 2 * PAD, :] = jnp.zeros((2, PAD, rows), jnp.float32)
        part = rows // 2
        start = pl.multiple_of(place_ref[0] * part, part)
        flat_ref[pl.ds(start, part), :] = mine_ref[...]
        flat_ref[pl.ds(pl.multiple_of(part - start, part), part), :] = other_half_ref[...]
        for c in range(tiles):
            weight_ref[tile_of(c)] = flat_ref[:, tile_of(c)].T

        def power_date(d, carry):
            for c in range(tiles):
                real, imag = slc_ref[d, 0, tile_of(c)], slc_ref[d, 1, tile_of(c)]
                field_ref[0, PAD + c * LANES : PAD + (c + 1) * LANES] = weight_ref[tile_of(c)] * (real * real + imag * imag)
            put_column_sums(field_ref.at[0], sums_ref.at[0])
            valid = valid_ref[d] != 0
            for n in range(0, cols, wide):
                columns = slice(n, n + wide)
                power = looked(sums_ref.at[0], band_ref, half_ref[:, columns], columns)
                inverse_ref[d, :, columns] = jnp.where(valid, lax.rsqrt(power), 0.0)
            return carry

        lax.fori_loop(0, dates_dev + REACH, power_date, 0)

    for c in range(0, cols, 4 * CHUNK):
        here = slice(c, c + 4 * CHUNK)
        weight = weight_ref[here]
        real, imag = weight * slc_ref[date, 0, here], weight * slc_ref[date, 1, here]
        far_real, far_imag = slc_ref[far, 0, here], slc_ref[far, 1, here]
        there = slice(PAD + c, PAD + c + 4 * CHUNK)
        field_ref[0, there] = real * far_real + imag * far_imag
        field_ref[1, there] = imag * far_real - real * far_imag
    for part in range(2):
        put_column_sums(field_ref.at[part], sums_ref.at[part])

    for n in range(0, cols, wide):
        columns = slice(n, n + wide)
        half = half_ref[:, columns]
        scale = inverse_ref[date, :, columns] * inverse_ref[far, :, columns]
        for part in range(2):
            unit = looked(sums_ref.at[part], band_ref, half, columns) * scale
            for k in range(wide // LANES):
                unit_ref[part, n // LANES + k, PAD : rows + PAD, :] = unit[:, tile_of(k)]

    for row in range(0, rows, CHUNK):
        units, means = [], []
        for part in range(2):
            centre = [unit_ref[part, c, row + PAD : row + PAD + CHUNK, :] for c in range(tiles)]
            column = [
                centre[c]
                + unit_ref[part, c, row + PAD - 1 : row + PAD - 1 + CHUNK, :]
                + unit_ref[part, c, row + PAD + 1 : row + PAD + 1 + CHUNK, :]
                for c in range(tiles)
            ]
            after, before = beside(column, 1), beside(column, -1)
            units.append(centre)
            means.append([(m + a + b) * (1.0 / 9.0) for m, a, b in zip(column, after, before)])
        for c in range(tiles):
            real, imag = units[0][c], units[1][c]
            gamma = jnp.sqrt(real * real + imag * imag)
            for part in range(2):
                mean = means[part][c]
                value = mean + gamma * (units[part][c] - mean)
                filtered_ref[0, 0, part, row : row + CHUNK, tile_of(c)] = value.astype(jnp.bfloat16)
            gamma_ref[0, 0, row : row + CHUNK, tile_of(c)] = gamma.astype(jnp.bfloat16)


def band_of(rows):
    gap = np.abs(np.arange(rows)[:, None] - np.arange(rows)[None, :])
    band = np.stack([(gap <= h).astype(np.float32) for h in (1, 2, 3)])
    return jnp.asarray(np.concatenate([band, band], axis=2), jnp.bfloat16)


def interferograms(place, slc, weights, look_half, slot, valid):
    ext, _, cols, rows = slc.shape
    dates_dev = ext - REACH
    whole = pl.BlockSpec(memory_space=pltpu.VMEM)
    spec = pltpu.PrefetchScalarGridSpec(
        num_scalar_prefetch=3,
        grid=(dates_dev * REACH,),
        in_specs=[whole] * 5,
        out_specs=[
            pl.BlockSpec((1, 1, 2, rows, cols), lambda s, slot, valid, place: (s // REACH, slot[s], 0, 0, 0)),
            pl.BlockSpec((1, 1, rows, cols), lambda s, slot, valid, place: (s // REACH, slot[s], 0, 0)),
        ],
        scratch_shapes=[
            pltpu.VMEM((rows, cols), jnp.float32),
            pltpu.VMEM((cols, rows), jnp.float32),
            pltpu.VMEM((ext, rows, cols), jnp.float32),
            pltpu.VMEM((2, cols + 2 * PAD, rows), jnp.float32),
            pltpu.VMEM((2, 3, cols, 2 * rows), jnp.bfloat16),
            pltpu.VMEM((2, cols // LANES, rows + 2 * PAD, LANES), jnp.float32),
        ],
    )
    return pl.pallas_call(
        functools.partial(main_kernel, dates_dev),
        grid_spec=spec,
        out_shape=[
            jax.ShapeDtypeStruct((dates_dev, REACH, 2, rows, cols), jnp.bfloat16),
            jax.ShapeDtypeStruct((dates_dev, REACH, rows, cols), jnp.bfloat16),
        ],
        compiler_params=pltpu.CompilerParams(vmem_limit_bytes=24 * 2**20),
        cost_estimate=pl.CostEstimate(flops=10**10, bytes_accessed=2 * 10**7, transcendentals=10**6),
    )(slot, valid, place, slc, *weights, look_half, band_of(rows))


def send(value, pairs):
    return lax.ppermute(value, "date", pairs)


def spread_weight(first, second, total_dates):
    return 1.0 / (1.0 + DISP_GAIN * (total_dates * second / (first * first) - 1.0))


def local(amplitude, phase, offset_code, look_half):
    dates_dev, rows, cols = amplitude.shape
    count = lax.axis_size("date")
    chips = count // 2
    total_dates = dates_dev * count
    index = lax.axis_index("date")
    place = jnp.stack([index % 2, index // 2]).astype(jnp.int32)
    mate_pairs = [(i, i ^ 1) for i in range(count)]
    to_even = [(i, i - 1) for i in range(1, count, 2)]
    next_pairs = [(i, i - 2) for i in range(2, count)]
    last_pairs = [(i, i - 3) for i in range(4, count, 2)]
    groups = [[core + 2 * chip for chip in range(chips)] for core in range(2)]

    amp_mate = send(amplitude, mate_pairs)
    pieces, early = moment_pieces(place, amplitude, amp_mate, phase, chips)
    moments = jnp.sum(lax.all_to_all(pieces, "date", 0, 0, axis_index_groups=groups), axis=0)
    following = [send(x, next_pairs) for x in (amplitude, phase)]
    last = send(early, last_pairs)
    phase_mate = send(phase, to_even)
    weight = spread_weight(moments[0], moments[1], total_dates)
    copies = jnp.broadcast_to(weight[None], (chips,) + weight.shape)
    mine = lax.all_to_all(copies, "date", 0, 0, axis_index_groups=groups).reshape(rows // 2, cols)
    following = after(following, copies)
    via = [send(x, mate_pairs) for x in following]
    weights = (mine, send(mine, mate_pairs))
    near = slc_turned(first_slc_kernel, place, amplitude, phase, *following)
    slc = slc_turned(second_slc_kernel, place, amp_mate, phase_mate, *via, last, begun=near)
    valid = (index * dates_dev + jnp.arange(dates_dev + REACH) < total_dates).astype(jnp.int32)
    same = offset_code[:, None, :] == jnp.arange(REACH, dtype=jnp.int32)[None, :, None]
    slot = jnp.sum(jnp.where(same, jnp.arange(REACH, dtype=jnp.int32), 0), axis=2, dtype=jnp.int32).reshape(-1)
    filtered, coherence = interferograms(place, slc, weights, look_half, slot, valid)
    return filtered, coherence


def solution(mesh):
    return jax.shard_map(
        local,
        mesh=mesh,
        in_specs=(P("date", "grp", None), P("date", "grp", None), P("date", None), P("grp", None)),
        out_specs=(P("date", None, None, "grp", None), P("date", None, "grp", None)),
        check_vma=False,
    )
```

```python
import functools

import jax
import jax.numpy as jnp
import numpy as np
from jax import lax
from jax.experimental import pallas as pl
from jax.experimental.pallas import tpu as pltpu
from jax.sharding import PartitionSpec as P

REACH = 5
DISP_GAIN = 4.0
LANES = 128
CHUNK = 16
PAD = 8

SIN_TERMS = (0.999999995714, -0.166666579612, 0.00833305031531, -0.000198090186189, 2.60509358011e-06)
COS_TERMS = (0.99999999978, -0.499999993556, 0.0416666361503, -0.00138883600009, 2.47600883899e-05, -2.60501805941e-07)


def series(square, terms):
    total = jnp.full_like(square, terms[-1])
    for term in terms[-2::-1]:
        total = total * square + term
    return total


def slc_of(amplitude, phase):
    amplitude = amplitude.astype(jnp.float32)
    half = phase.astype(jnp.float32) * 0.5
    square = half * half
    sine = half * series(square, SIN_TERMS)
    cosine = series(square, COS_TERMS)
    scaled = (amplitude + amplitude) * sine
    return amplitude - scaled * sine, scaled * cosine


def over_rows(rows, body):
    def step(index, carry):
        body(pl.ds(pl.multiple_of(index * CHUNK, CHUNK), CHUNK))
        return carry

    lax.fori_loop(0, rows // CHUNK, step, 0)


def cost(pixels, flops, nbytes):
    return pl.CostEstimate(flops=pixels * flops, bytes_accessed=pixels * nbytes, transcendentals=0)


VMEM = pl.BlockSpec(memory_space=pltpu.VMEM)
SMEM = pl.BlockSpec(memory_space=pltpu.SMEM)


def slc_dates(place_ref, sources, slc_ref):
    odd = place_ref[0] != 0

    def body(n, carry):
        columns = pl.ds(pl.multiple_of(n * LANES, LANES), LANES)
        for date, pair, index, other, other_index in sources:
            found = []
            for k in range(2):
                value = pair[k][index, :, columns].astype(jnp.float32)
                if other is not None:
                    value = jnp.where(odd, value, other[k][other_index, :, columns].astype(jnp.float32))
                found.append(value.T)
            slc_ref[date, 0, columns], slc_ref[date, 1, columns] = slc_of(*found)
        return carry

    lax.fori_loop(0, sources[0][1][0].shape[2] // LANES, body, 0)


def first_slc_kernel(place_ref, own_amp, own_phase, next_amp, next_phase, slc_ref):
    own, following = (own_amp, own_phase), (next_amp, next_phase)
    slc_dates(
        place_ref,
        [(0, own, 0, None, 0), (1, own, 1, None, 0), (4, following, 0, None, 0), (5, following, 1, None, 0)],
        slc_ref,
    )


def second_slc_kernel(place_ref, mate_amp, mate_phase, via_amp, via_phase, last_ref, begun_ref, slc_ref):
    mate, via, last = (mate_amp, mate_phase), (via_amp, via_phase), (last_ref.at[0:1], last_ref.at[1:2])
    slc_dates(place_ref, [(2, via, 0, mate, 0), (3, via, 1, mate, 1), (6, last, 0, via, 0)], slc_ref)


def slc_turned(kernel, place, *arrays, begun=None):
    dates, rows, cols = arrays[0].shape
    if begun is not None:
        arrays = arrays + (begun,)
    return pl.pallas_call(
        kernel,
        in_specs=[SMEM] + [VMEM] * len(arrays),
        out_specs=VMEM,
        out_shape=jax.ShapeDtypeStruct((dates + REACH, 2, cols, rows), jnp.float32),
        input_output_aliases={} if begun is None else {len(arrays): 0},
        compiler_params=pltpu.CompilerParams(vmem_limit_bytes=16 * 2**20),
        cost_estimate=cost(dates * rows * cols, 8000, 12),
    )(place, *arrays)


def gate_kernel(*refs):
    pass


def after(values, *others):
    ANY = pl.BlockSpec(memory_space=pl.ANY)
    return pl.pallas_call(
        gate_kernel,
        in_specs=[ANY] * (len(values) + len(others)),
        out_specs=[ANY] * len(values),
        out_shape=[jax.ShapeDtypeStruct(v.shape, v.dtype) for v in values],
        input_output_aliases={k: k for k in range(len(values))},
    )(*values, *others)


def moments_kernel(place_ref, own_ref, mate_ref, phase_ref, pieces_ref, early_ref):
    chips, _, deep, cols = pieces_ref.shape
    half = chips * deep
    start = place_ref[0] * half
    early_ref[0] = own_ref[0]
    early_ref[1] = phase_ref[0]

    for row in range(0, half, CHUNK):
        there = pl.ds(pl.multiple_of(start + row, CHUNK), CHUNK)
        values = [ref[d, there].astype(jnp.float32) for ref in (own_ref, mate_ref) for d in range(ref.shape[0])]
        squares = [v * v for v in values]
        for which, total in enumerate((sum(values[1:], values[0]), sum(squares[1:], squares[0]))):
            for low in range(0, CHUNK, min(deep, CHUNK)):
                chip, inside = (row + low) // deep, (row + low) % deep
                size = min(deep, CHUNK)
                pieces_ref[chip, which, inside : inside + size] = total[low : low + size]


def moment_pieces(place, own, mate, phase, chips):
    _, rows, cols = own.shape
    half = rows // 2
    return pl.pallas_call(
        moments_kernel,
        in_specs=[SMEM, VMEM, VMEM, VMEM],
        out_specs=[VMEM, VMEM],
        out_shape=[
            jax.ShapeDtypeStruct((chips, 2, half // chips, cols), jnp.float32),
            jax.ShapeDtypeStruct((2, rows, cols), jnp.bfloat16),
        ],
        cost_estimate=cost(half * cols, 12, 24),
    )(place, own, mate, phase)


def beside(tiles, step):
    lane = lax.broadcasted_iota(jnp.int32, tiles[0].shape, 1)
    turned = [pltpu.roll(tile, (-step) % LANES, 1) for tile in tiles]
    count = len(tiles)
    out = []
    for c in range(count):
        if step > 0:
            other = turned[c + 1] if c + 1 < count else jnp.zeros_like(tiles[0])
            out.append(jnp.where(lane >= LANES - step, other, turned[c]))
        else:
            other = turned[c - 1] if c > 0 else jnp.zeros_like(tiles[0])
            out.append(jnp.where(lane < -step, other, turned[c]))
    return out


def put_column_sums(field_ref, sums_ref):
    cols, rows = sums_ref.shape[1], sums_ref.shape[2] // 2
    for c in range(0, cols, CHUNK):
        total = field_ref[PAD + c : PAD + c + CHUNK]
        for j in (1, 2, 3):
            total = total + (field_ref[PAD + c + j : PAD + c + j + CHUNK] + field_ref[PAD + c - j : PAD + c - j + CHUNK])
            high = total.astype(jnp.bfloat16)
            sums_ref[j - 1, c : c + CHUNK, :rows] = high
            sums_ref[j - 1, c : c + CHUNK, rows:] = (total - high.astype(jnp.float32)).astype(jnp.bfloat16)


def looked(sums_ref, band_ref, half, columns):
    box = [
        lax.dot_general(band_ref[h], sums_ref[h, columns, :], (((1,), (1,)), ((), ())), preferred_element_type=jnp.float32)
        for h in range(3)
    ]
    return jnp.where(half == 1, box[0], jnp.where(half == 2, box[1], box[2]))


def main_kernel(
    dates_dev, slot_ref, valid_ref, place_ref, slc_ref, mine_ref, other_half_ref, half_ref, band_ref,
    filtered_ref, gamma_ref, flat_ref, weight_ref, inverse_ref, field_ref, sums_ref, unit_ref,
):
    cols, rows = weight_ref.shape
    tiles = cols // LANES
    wide = 2 * LANES
    step = pl.program_id(0)
    date = step // REACH
    far = date + step % REACH + 1

    def tile_of(c):
        return slice(c * LANES, (c + 1) * LANES)

    @pl.when(step == 0)
    def _():
        unit_ref[:, :, 0:PAD, :] = jnp.zeros((2, tiles, PAD, LANES), jnp.float32)
        unit_ref[:, :, rows + PAD : rows + 2 * PAD, :] = jnp.zeros((2, tiles, PAD, LANES), jnp.float32)
        field_ref[:, 0:PAD, :] = jnp.zeros((2, PAD, rows), jnp.float32)
        field_ref[:, cols + PAD : cols + 2 * PAD, :] = jnp.zeros((2, PAD, rows), jnp.float32)
        part = rows // 2
        start = pl.multiple_of(place_ref[0] * part, part)
        flat_ref[pl.ds(start, part), :] = mine_ref[...]
        flat_ref[pl.ds(pl.multiple_of(part - start, part), part), :] = other_half_ref[...]
        for c in range(tiles):
            weight_ref[tile_of(c)] = flat_ref[:, tile_of(c)].T

        def power_date(d, carry):
            for c in range(tiles):
                real, imag = slc_ref[d, 0, tile_of(c)], slc_ref[d, 1, tile_of(c)]
                field_ref[0, PAD + c * LANES : PAD + (c + 1) * LANES] = weight_ref[tile_of(c)] * (real * real + imag * imag)
            put_column_sums(field_ref.at[0], sums_ref.at[0])
            valid = valid_ref[d] != 0
            for n in range(0, cols, wide):
                columns = slice(n, n + wide)
                power = looked(sums_ref.at[0], band_ref, half_ref[:, columns], columns)
                inverse_ref[d, :, columns] = jnp.where(valid, lax.rsqrt(power), 0.0)
            return carry

        lax.fori_loop(0, dates_dev + REACH, power_date, 0)

    for c in range(0, cols, 4 * CHUNK):
        here = slice(c, c + 4 * CHUNK)
        weight = weight_ref[here]
        real, imag = weight * slc_ref[date, 0, here], weight * slc_ref[date, 1, here]
        far_real, far_imag = slc_ref[far, 0, here], slc_ref[far, 1, here]
        there = slice(PAD + c, PAD + c + 4 * CHUNK)
        field_ref[0, there] = real * far_real + imag * far_imag
        field_ref[1, there] = imag * far_real - real * far_imag
    for part in range(2):
        put_column_sums(field_ref.at[part], sums_ref.at[part])

    for n in range(0, cols, wide):
        columns = slice(n, n + wide)
        half = half_ref[:, columns]
        scale = inverse_ref[date, :, columns] * inverse_ref[far, :, columns]
        for part in range(2):
            unit = looked(sums_ref.at[part], band_ref, half, columns) * scale
            for k in range(wide // LANES):
                unit_ref[part, n // LANES + k, PAD : rows + PAD, :] = unit[:, tile_of(k)]

    for row in range(0, rows, CHUNK):
        units, means = [], []
        for part in range(2):
            centre = [unit_ref[part, c, row + PAD : row + PAD + CHUNK, :] for c in range(tiles)]
            column = [
                centre[c]
                + unit_ref[part, c, row + PAD - 1 : row + PAD - 1 + CHUNK, :]
                + unit_ref[part, c, row + PAD + 1 : row + PAD + 1 + CHUNK, :]
                for c in range(tiles)
            ]
            after, before = beside(column, 1), beside(column, -1)
            units.append(centre)
            means.append([(m + a + b) * (1.0 / 9.0) for m, a, b in zip(column, after, before)])
        for c in range(tiles):
            real, imag = units[0][c], units[1][c]
            gamma = jnp.sqrt(real * real + imag * imag)
            for part in range(2):
                mean = means[part][c]
                value = mean + gamma * (units[part][c] - mean)
                filtered_ref[0, 0, part, row : row + CHUNK, tile_of(c)] = value.astype(jnp.bfloat16)
            gamma_ref[0, 0, row : row + CHUNK, tile_of(c)] = gamma.astype(jnp.bfloat16)


def band_of(rows):
    gap = np.abs(np.arange(rows)[:, None] - np.arange(rows)[None, :])
    band = np.stack([(gap <= h).astype(np.float32) for h in (1, 2, 3)])
    return jnp.asarray(np.concatenate([band, band], axis=2), jnp.bfloat16)


def interferograms(place, slc, weights, look_half, slot, valid):
    ext, _, cols, rows = slc.shape
    dates_dev = ext - REACH
    whole = pl.BlockSpec(memory_space=pltpu.VMEM)
    spec = pltpu.PrefetchScalarGridSpec(
        num_scalar_prefetch=3,
        grid=(dates_dev * REACH,),
        in_specs=[whole] * 5,
        out_specs=[
            pl.BlockSpec((1, 1, 2, rows, cols), lambda s, slot, valid, place: (s // REACH, slot[s], 0, 0, 0)),
            pl.BlockSpec((1, 1, rows, cols), lambda s, slot, valid, place: (s // REACH, slot[s], 0, 0)),
        ],
        scratch_shapes=[
            pltpu.VMEM((rows, cols), jnp.float32),
            pltpu.VMEM((cols, rows), jnp.float32),
            pltpu.VMEM((ext, rows, cols), jnp.float32),
            pltpu.VMEM((2, cols + 2 * PAD, rows), jnp.float32),
            pltpu.VMEM((2, 3, cols, 2 * rows), jnp.bfloat16),
            pltpu.VMEM((2, cols // LANES, rows + 2 * PAD, LANES), jnp.float32),
        ],
    )
    return pl.pallas_call(
        functools.partial(main_kernel, dates_dev),
        grid_spec=spec,
        out_shape=[
            jax.ShapeDtypeStruct((dates_dev, REACH, 2, rows, cols), jnp.bfloat16),
            jax.ShapeDtypeStruct((dates_dev, REACH, rows, cols), jnp.bfloat16),
        ],
        compiler_params=pltpu.CompilerParams(vmem_limit_bytes=24 * 2**20),
        cost_estimate=pl.CostEstimate(flops=10**10, bytes_accessed=2 * 10**7, transcendentals=10**6),
    )(slot, valid, place, slc, *weights, look_half, band_of(rows))


def send(value, pairs):
    return lax.ppermute(value, "date", pairs)


def spread_weight(first, second, total_dates):
    return 1.0 / (1.0 + DISP_GAIN * (total_dates * second / (first * first) - 1.0))


def local(amplitude, phase, offset_code, look_half):
    dates_dev, rows, cols = amplitude.shape
    count = lax.axis_size("date")
    chips = count // 2
    total_dates = dates_dev * count
    index = lax.axis_index("date")
    place = jnp.stack([index % 2, index // 2]).astype(jnp.int32)
    mate_pairs = [(i, i ^ 1) for i in range(count)]
    to_even = [(i, i - 1) for i in range(1, count, 2)]
    next_pairs = [(i, i - 2) for i in range(2, count)]
    last_pairs = [(i, i - 3) for i in range(4, count, 2)]
    groups = [[core + 2 * chip for chip in range(chips)] for core in range(2)]

    amp_mate = send(amplitude, mate_pairs)
    pieces, early = moment_pieces(place, amplitude, amp_mate, phase, chips)
    moments = jnp.sum(lax.all_to_all(pieces, "date", 0, 0, axis_index_groups=groups), axis=0)
    following = [send(x, next_pairs) for x in (amplitude, phase)]
    last = send(early, last_pairs)
    phase_mate = send(phase, to_even)
    weight = spread_weight(moments[0], moments[1], total_dates)
    copies = jnp.broadcast_to(weight[None], (chips,) + weight.shape)
    mine = lax.all_to_all(copies, "date", 0, 0, axis_index_groups=groups).reshape(rows // 2, cols)
    following = after(following, copies)
    via = [send(x, mate_pairs) for x in following]
    weights = (mine, send(mine, mate_pairs))
    near = slc_turned(first_slc_kernel, place, amplitude, phase, *following)
    slc = slc_turned(second_slc_kernel, place, amp_mate, phase_mate, *via, last, begun=near)
    valid = (index * dates_dev + jnp.arange(dates_dev + REACH) < total_dates).astype(jnp.int32)
    same = offset_code[:, None, :] == jnp.arange(REACH, dtype=jnp.int32)[None, :, None]
    slot = jnp.sum(jnp.where(same, jnp.arange(REACH, dtype=jnp.int32), 0), axis=2, dtype=jnp.int32).reshape(-1)
    filtered, coherence = interferograms(place, slc, weights, look_half, slot, valid)
    return filtered, coherence


def solution(mesh):
    return jax.shard_map(
        local,
        mesh=mesh,
        in_specs=(P("date", "grp", None), P("date", "grp", None), P("date", None), P("grp", None)),
        out_specs=(P("date", None, None, "grp", None), P("date", None, "grp", None)),
        check_vma=False,
    )
```

```python
import functools

import jax
import jax.numpy as jnp
import numpy as np
from jax import lax
from jax.experimental import pallas as pl
from jax.experimental.pallas import tpu as pltpu
from jax.sharding import PartitionSpec as P

REACH = 5
DISP_GAIN = 4.0
LANES = 128
CHUNK = 16
PAD = 8

SIN_TERMS = (0.999999995714, -0.166666579612, 0.00833305031531, -0.000198090186189, 2.60509358011e-06)
COS_TERMS = (0.99999999978, -0.499999993556, 0.0416666361503, -0.00138883600009, 2.47600883899e-05, -2.60501805941e-07)


def series(square, terms):
    total = jnp.full_like(square, terms[-1])
    for term in terms[-2::-1]:
        total = total * square + term
    return total


def slc_of(amplitude, phase):
    amplitude = amplitude.astype(jnp.float32)
    half = phase.astype(jnp.float32) * 0.5
    square = half * half
    sine = half * series(square, SIN_TERMS)
    cosine = series(square, COS_TERMS)
    scaled = (amplitude + amplitude) * sine
    return amplitude - scaled * sine, scaled * cosine


def over_rows(rows, body):
    def step(index, carry):
        body(pl.ds(pl.multiple_of(index * CHUNK, CHUNK), CHUNK))
        return carry

    lax.fori_loop(0, rows // CHUNK, step, 0)


def cost(pixels, flops, nbytes):
    return pl.CostEstimate(flops=pixels * flops, bytes_accessed=pixels * nbytes, transcendentals=0)


VMEM = pl.BlockSpec(memory_space=pltpu.VMEM)
SMEM = pl.BlockSpec(memory_space=pltpu.SMEM)


def slc_dates(sources, slc_ref):
    odd = lax.axis_index("date") % 2 != 0

    def body(n, carry):
        columns = pl.ds(pl.multiple_of(n * LANES, LANES), LANES)
        for date, pair, index, other, other_index in sources:
            found = []
            for k in range(2):
                value = pair[k][index, :, columns].astype(jnp.float32)
                if other is not None:
                    value = jnp.where(odd, value, other[k][other_index, :, columns].astype(jnp.float32))
                found.append(value.T)
            slc_ref[date, 0, columns], slc_ref[date, 1, columns] = slc_of(*found)
        return carry

    lax.fori_loop(0, sources[0][1][0].shape[2] // LANES, body, 0)


def first_slc_kernel(next_amp, next_phase, slc_ref):
    following = (next_amp, next_phase)
    slc_dates([(4, following, 0, None, 0), (5, following, 1, None, 0)], slc_ref)


def second_slc_kernel(
    mate_amp, mate_phase, via_amp, via_phase, last_ref, own_amp, own_phase, begun_ref, slc_ref
):
    own, mate, via = (own_amp, own_phase), (mate_amp, mate_phase), (via_amp, via_phase)
    last = (last_ref.at[0:1], last_ref.at[1:2])
    sources = [(0, own, 0, None, 0), (1, own, 1, None, 0)]
    sources += [(2, via, 0, mate, 0), (3, via, 1, mate, 1), (6, last, 0, via, 0)]
    slc_dates(sources, slc_ref)


def slc_turned(kernel, *arrays, begun=None):
    dates, rows, cols = arrays[0].shape
    if begun is not None:
        arrays = arrays + (begun,)
    return pl.pallas_call(
        kernel,
        in_specs=[VMEM] * len(arrays),
        out_specs=VMEM,
        out_shape=jax.ShapeDtypeStruct((dates + REACH, 2, cols, rows), jnp.float32),
        input_output_aliases={} if begun is None else {len(arrays) - 1: 0},
        compiler_params=pltpu.CompilerParams(vmem_limit_bytes=16 * 2**20),
        cost_estimate=cost(dates * rows * cols, 8000, 12),
    )(*arrays)


def gate_kernel(*refs):
    pass


def after(values, *others):
    ANY = pl.BlockSpec(memory_space=pl.ANY)
    return pl.pallas_call(
        gate_kernel,
        in_specs=[ANY] * (len(values) + len(others)),
        out_specs=[ANY] * len(values),
        out_shape=[jax.ShapeDtypeStruct(v.shape, v.dtype) for v in values],
        input_output_aliases={k: k for k in range(len(values))},
    )(*values, *others)


def moments_kernel(place_ref, own_ref, mate_ref, phase_ref, pieces_ref, early_ref):
    chips, _, deep, cols = pieces_ref.shape
    half = chips * deep
    start = place_ref[0] * half
    early_ref[0] = own_ref[0]
    early_ref[1] = phase_ref[0]

    for row in range(0, half, CHUNK):
        there = pl.ds(pl.multiple_of(start + row, CHUNK), CHUNK)
        values = [ref[d, there].astype(jnp.float32) for ref in (own_ref, mate_ref) for d in range(ref.shape[0])]
        squares = [v * v for v in values]
        for which, total in enumerate((sum(values[1:], values[0]), sum(squares[1:], squares[0]))):
            for low in range(0, CHUNK, min(deep, CHUNK)):
                chip, inside = (row + low) // deep, (row + low) % deep
                size = min(deep, CHUNK)
                pieces_ref[chip, which, inside : inside + size] = total[low : low + size]


def moment_pieces(place, own, mate, phase, chips):
    _, rows, cols = own.shape
    half = rows // 2
    return pl.pallas_call(
        moments_kernel,
        in_specs=[SMEM, VMEM, VMEM, VMEM],
        out_specs=[VMEM, VMEM],
        out_shape=[
            jax.ShapeDtypeStruct((chips, 2, half // chips, cols), jnp.float32),
            jax.ShapeDtypeStruct((2, rows, cols), jnp.bfloat16),
        ],
        cost_estimate=cost(half * cols, 12, 24),
    )(place, own, mate, phase)


def beside(tiles, step):
    lane = lax.broadcasted_iota(jnp.int32, tiles[0].shape, 1)
    turned = [pltpu.roll(tile, (-step) % LANES, 1) for tile in tiles]
    count = len(tiles)
    out = []
    for c in range(count):
        if step > 0:
            other = turned[c + 1] if c + 1 < count else jnp.zeros_like(tiles[0])
            out.append(jnp.where(lane >= LANES - step, other, turned[c]))
        else:
            other = turned[c - 1] if c > 0 else jnp.zeros_like(tiles[0])
            out.append(jnp.where(lane < -step, other, turned[c]))
    return out


def put_column_sums(field_ref, sums_ref):
    cols, rows = sums_ref.shape[1], sums_ref.shape[2] // 2
    for c in range(0, cols, CHUNK):
        total = field_ref[PAD + c : PAD + c + CHUNK]
        for j in (1, 2, 3):
            total = total + (field_ref[PAD + c + j : PAD + c + j + CHUNK] + field_ref[PAD + c - j : PAD + c - j + CHUNK])
            high = total.astype(jnp.bfloat16)
            sums_ref[j - 1, c : c + CHUNK, :rows] = high
            sums_ref[j - 1, c : c + CHUNK, rows:] = (total - high.astype(jnp.float32)).astype(jnp.bfloat16)


def looked(sums_ref, band_ref, half, columns):
    box = [
        lax.dot_general(band_ref[h], sums_ref[h, columns, :], (((1,), (1,)), ((), ())), preferred_element_type=jnp.float32)
        for h in range(3)
    ]
    return jnp.where(half == 1, box[0], jnp.where(half == 2, box[1], box[2]))


def main_kernel(
    dates_dev, slot_ref, valid_ref, place_ref, slc_ref, mine_ref, other_half_ref, half_ref, band_ref,
    filtered_ref, gamma_ref, flat_ref, weight_ref, inverse_ref, field_ref, sums_ref, unit_ref,
):
    cols, rows = weight_ref.shape
    tiles = cols // LANES
    wide = 2 * LANES
    step = pl.program_id(0)
    date = step // REACH
    far = date + step % REACH + 1

    def tile_of(c):
        return slice(c * LANES, (c + 1) * LANES)

    @pl.when(step == 0)
    def _():
        unit_ref[:, :, 0:PAD, :] = jnp.zeros((2, tiles, PAD, LANES), jnp.float32)
        unit_ref[:, :, rows + PAD : rows + 2 * PAD, :] = jnp.zeros((2, tiles, PAD, LANES), jnp.float32)
        field_ref[:, 0:PAD, :] = jnp.zeros((2, PAD, rows), jnp.float32)
        field_ref[:, cols + PAD : cols + 2 * PAD, :] = jnp.zeros((2, PAD, rows), jnp.float32)
        part = rows // 2
        start = pl.multiple_of(place_ref[0] * part, part)
        flat_ref[pl.ds(start, part), :] = mine_ref[...]
        flat_ref[pl.ds(pl.multiple_of(part - start, part), part), :] = other_half_ref[...]
        for c in range(tiles):
            weight_ref[tile_of(c)] = flat_ref[:, tile_of(c)].T

        def power_date(d, carry):
            for c in range(tiles):
                real, imag = slc_ref[d, 0, tile_of(c)], slc_ref[d, 1, tile_of(c)]
                field_ref[0, PAD + c * LANES : PAD + (c + 1) * LANES] = weight_ref[tile_of(c)] * (real * real + imag * imag)
            put_column_sums(field_ref.at[0], sums_ref.at[0])
            valid = valid_ref[d] != 0
            for n in range(0, cols, wide):
                columns = slice(n, n + wide)
                power = looked(sums_ref.at[0], band_ref, half_ref[:, columns], columns)
                inverse_ref[d, :, columns] = jnp.where(valid, lax.rsqrt(power), 0.0)
            return carry

        lax.fori_loop(0, dates_dev + REACH, power_date, 0)

    for c in range(0, cols, 4 * CHUNK):
        here = slice(c, c + 4 * CHUNK)
        weight = weight_ref[here]
        real, imag = weight * slc_ref[date, 0, here], weight * slc_ref[date, 1, here]
        far_real, far_imag = slc_ref[far, 0, here], slc_ref[far, 1, here]
        there = slice(PAD + c, PAD + c + 4 * CHUNK)
        field_ref[0, there] = real * far_real + imag * far_imag
        field_ref[1, there] = imag * far_real - real * far_imag
    for part in range(2):
        put_column_sums(field_ref.at[part], sums_ref.at[part])

    for n in range(0, cols, wide):
        columns = slice(n, n + wide)
        half = half_ref[:, columns]
        scale = inverse_ref[date, :, columns] * inverse_ref[far, :, columns]
        for part in range(2):
            unit = looked(sums_ref.at[part], band_ref, half, columns) * scale
            for k in range(wide // LANES):
                unit_ref[part, n // LANES + k, PAD : rows + PAD, :] = unit[:, tile_of(k)]

    for row in range(0, rows, CHUNK):
        units, means = [], []
        for part in range(2):
            centre = [unit_ref[part, c, row + PAD : row + PAD + CHUNK, :] for c in range(tiles)]
            column = [
                centre[c]
                + unit_ref[part, c, row + PAD - 1 : row + PAD - 1 + CHUNK, :]
                + unit_ref[part, c, row + PAD + 1 : row + PAD + 1 + CHUNK, :]
                for c in range(tiles)
            ]
            after, before = beside(column, 1), beside(column, -1)
            units.append(centre)
            means.append([(m + a + b) * (1.0 / 9.0) for m, a, b in zip(column, after, before)])
        for c in range(tiles):
            real, imag = units[0][c], units[1][c]
            gamma = jnp.sqrt(real * real + imag * imag)
            for part in range(2):
                mean = means[part][c]
                value = mean + gamma * (units[part][c] - mean)
                filtered_ref[0, 0, part, row : row + CHUNK, tile_of(c)] = value.astype(jnp.bfloat16)
            gamma_ref[0, 0, row : row + CHUNK, tile_of(c)] = gamma.astype(jnp.bfloat16)


def band_of(rows):
    gap = np.abs(np.arange(rows)[:, None] - np.arange(rows)[None, :])
    band = np.stack([(gap <= h).astype(np.float32) for h in (1, 2, 3)])
    return jnp.asarray(np.concatenate([band, band], axis=2), jnp.bfloat16)


def interferograms(place, slc, weights, look_half, slot, valid):
    ext, _, cols, rows = slc.shape
    dates_dev = ext - REACH
    whole = pl.BlockSpec(memory_space=pltpu.VMEM)
    spec = pltpu.PrefetchScalarGridSpec(
        num_scalar_prefetch=3,
        grid=(dates_dev * REACH,),
        in_specs=[whole] * 5,
        out_specs=[
            pl.BlockSpec((1, 1, 2, rows, cols), lambda s, slot, valid, place: (s // REACH, slot[s], 0, 0, 0)),
            pl.BlockSpec((1, 1, rows, cols), lambda s, slot, valid, place: (s // REACH, slot[s], 0, 0)),
        ],
        scratch_shapes=[
            pltpu.VMEM((rows, cols), jnp.float32),
            pltpu.VMEM((cols, rows), jnp.float32),
            pltpu.VMEM((ext, rows, cols), jnp.float32),
            pltpu.VMEM((2, cols + 2 * PAD, rows), jnp.float32),
            pltpu.VMEM((2, 3, cols, 2 * rows), jnp.bfloat16),
            pltpu.VMEM((2, cols // LANES, rows + 2 * PAD, LANES), jnp.float32),
        ],
    )
    return pl.pallas_call(
        functools.partial(main_kernel, dates_dev),
        grid_spec=spec,
        out_shape=[
            jax.ShapeDtypeStruct((dates_dev, REACH, 2, rows, cols), jnp.bfloat16),
            jax.ShapeDtypeStruct((dates_dev, REACH, rows, cols), jnp.bfloat16),
        ],
        compiler_params=pltpu.CompilerParams(vmem_limit_bytes=24 * 2**20),
        cost_estimate=pl.CostEstimate(flops=10**10, bytes_accessed=2 * 10**7, transcendentals=10**6),
    )(slot, valid, place, slc, *weights, look_half, band_of(rows))


def send(value, pairs):
    return lax.ppermute(value, "date", pairs)


def spread_weight(first, second, total_dates):
    return 1.0 / (1.0 + DISP_GAIN * (total_dates * second / (first * first) - 1.0))


def local(amplitude, phase, offset_code, look_half):
    dates_dev, rows, cols = amplitude.shape
    count = lax.axis_size("date")
    chips = count // 2
    total_dates = dates_dev * count
    index = lax.axis_index("date")
    place = jnp.stack([index % 2, index // 2]).astype(jnp.int32)
    mate_pairs = [(i, i ^ 1) for i in range(count)]
    to_even = [(i, i - 1) for i in range(1, count, 2)]
    next_pairs = [(i, i - 2) for i in range(2, count)]
    last_pairs = [(i, i - 3) for i in range(4, count, 2)]
    groups = [[core + 2 * chip for chip in range(chips)] for core in range(2)]

    amp_mate = send(amplitude, mate_pairs)
    pieces, early = moment_pieces(place, amplitude, amp_mate, phase, chips)
    moments = jnp.sum(lax.all_to_all(pieces, "date", 0, 0, axis_index_groups=groups), axis=0)
    following = [send(x, next_pairs) for x in (amplitude, phase)]
    last = send(early, last_pairs)
    phase_mate = send(phase, to_even)
    weight = spread_weight(moments[0], moments[1], total_dates)
    copies = jnp.broadcast_to(weight[None], (chips,) + weight.shape)
    mine = lax.all_to_all(copies, "date", 0, 0, axis_index_groups=groups).reshape(rows // 2, cols)
    following = after(following, copies)
    via = [send(x, mate_pairs) for x in following]
    weights = (mine, send(mine, mate_pairs))
    near = slc_turned(first_slc_kernel, *following)
    slc = slc_turned(second_slc_kernel, amp_mate, phase_mate, *via, last, amplitude, phase, begun=near)
    valid = (index * dates_dev + jnp.arange(dates_dev + REACH) < total_dates).astype(jnp.int32)
    same = offset_code[:, None, :] == jnp.arange(REACH, dtype=jnp.int32)[None, :, None]
    slot = jnp.sum(jnp.where(same, jnp.arange(REACH, dtype=jnp.int32), 0), axis=2, dtype=jnp.int32).reshape(-1)
    filtered, coherence = interferograms(place, slc, weights, look_half, slot, valid)
    return filtered, coherence


def solution(mesh):
    return jax.shard_map(
        local,
        mesh=mesh,
        in_specs=(P("date", "grp", None), P("date", "grp", None), P("date", None), P("grp", None)),
        out_specs=(P("date", None, None, "grp", None), P("date", None, "grp", None)),
        check_vma=False,
    )
```

```python
import functools

import jax
import jax.numpy as jnp
import numpy as np
from jax import lax
from jax.experimental import pallas as pl
from jax.experimental.pallas import tpu as pltpu
from jax.sharding import PartitionSpec as P

REACH = 5
DISP_GAIN = 4.0
LANES = 128
CHUNK = 16
PAD = 8

SIN_TERMS = (0.999999995714, -0.166666579612, 0.00833305031531, -0.000198090186189, 2.60509358011e-06)
COS_TERMS = (0.99999999978, -0.499999993556, 0.0416666361503, -0.00138883600009, 2.47600883899e-05, -2.60501805941e-07)


def series(square, terms):
    total = jnp.full_like(square, terms[-1])
    for term in terms[-2::-1]:
        total = total * square + term
    return total


def slc_of(amplitude, phase):
    amplitude = amplitude.astype(jnp.float32)
    half = phase.astype(jnp.float32) * 0.5
    square = half * half
    sine = half * series(square, SIN_TERMS)
    cosine = series(square, COS_TERMS)
    scaled = (amplitude + amplitude) * sine
    return amplitude - scaled * sine, scaled * cosine


def over_rows(rows, body):
    def step(index, carry):
        body(pl.ds(pl.multiple_of(index * CHUNK, CHUNK), CHUNK))
        return carry

    lax.fori_loop(0, rows // CHUNK, step, 0)


def cost(pixels, flops, nbytes):
    return pl.CostEstimate(flops=pixels * flops, bytes_accessed=pixels * nbytes, transcendentals=0)


VMEM = pl.BlockSpec(memory_space=pltpu.VMEM)
SMEM = pl.BlockSpec(memory_space=pltpu.SMEM)


def slc_dates(sources, slc_ref):
    odd = lax.axis_index("date") % 2 != 0

    def body(n, carry):
        columns = pl.ds(pl.multiple_of(n * LANES, LANES), LANES)
        for date, pair, index, other, other_index in sources:
            found = []
            for k in range(2):
                value = pair[k][index, :, columns].astype(jnp.float32)
                if other is not None:
                    value = jnp.where(odd, value, other[k][other_index, :, columns].astype(jnp.float32))
                found.append(value.T)
            slc_ref[date, 0, columns], slc_ref[date, 1, columns] = slc_of(*found)
        return carry

    lax.fori_loop(0, sources[0][1][0].shape[2] // LANES, body, 0)


def first_slc_kernel(next_amp, next_phase, slc_ref):
    following = (next_amp, next_phase)
    slc_dates([(4, following, 0, None, 0), (5, following, 1, None, 0)], slc_ref)


def second_slc_kernel(
    mate_amp, mate_phase, via_amp, via_phase, last_ref, own_amp, own_phase, begun_ref, slc_ref
):
    own, mate, via = (own_amp, own_phase), (mate_amp, mate_phase), (via_amp, via_phase)
    last = (last_ref.at[0:1], last_ref.at[1:2])
    sources = [(0, own, 0, None, 0), (1, own, 1, None, 0)]
    sources += [(2, via, 0, mate, 0), (3, via, 1, mate, 1), (6, last, 0, via, 0)]
    slc_dates(sources, slc_ref)


def slc_turned(kernel, *arrays, begun=None):
    dates, rows, cols = arrays[0].shape
    if begun is not None:
        arrays = arrays + (begun,)
    return pl.pallas_call(
        kernel,
        in_specs=[VMEM] * len(arrays),
        out_specs=VMEM,
        out_shape=jax.ShapeDtypeStruct((dates + REACH, 2, cols, rows), jnp.float32),
        input_output_aliases={} if begun is None else {len(arrays) - 1: 0},
        compiler_params=pltpu.CompilerParams(vmem_limit_bytes=16 * 2**20),
        cost_estimate=cost(dates * rows * cols, 8000, 12),
    )(*arrays)


def gate_kernel(*refs):
    pass


def after(values, *others):
    ANY = pl.BlockSpec(memory_space=pl.ANY)
    return pl.pallas_call(
        gate_kernel,
        in_specs=[ANY] * (len(values) + len(others)),
        out_specs=[ANY] * len(values),
        out_shape=[jax.ShapeDtypeStruct(v.shape, v.dtype) for v in values],
        input_output_aliases={k: k for k in range(len(values))},
    )(*values, *others)


def moments_kernel(place_ref, own_ref, mate_ref, phase_ref, pieces_ref, early_ref):
    chips, _, deep, cols = pieces_ref.shape
    half = chips * deep
    start = place_ref[0] * half
    early_ref[0] = own_ref[0]
    early_ref[1] = phase_ref[0]

    for row in range(0, half, CHUNK):
        there = pl.ds(pl.multiple_of(start + row, CHUNK), CHUNK)
        values = [ref[d, there].astype(jnp.float32) for ref in (own_ref, mate_ref) for d in range(ref.shape[0])]
        squares = [v * v for v in values]
        for which, total in enumerate((sum(values[1:], values[0]), sum(squares[1:], squares[0]))):
            for low in range(0, CHUNK, min(deep, CHUNK)):
                chip, inside = (row + low) // deep, (row + low) % deep
                size = min(deep, CHUNK)
                pieces_ref[chip, which, inside : inside + size] = total[low : low + size]


def moment_pieces(place, own, mate, phase, chips):
    _, rows, cols = own.shape
    half = rows // 2
    return pl.pallas_call(
        moments_kernel,
        in_specs=[SMEM, VMEM, VMEM, VMEM],
        out_specs=[VMEM, VMEM],
        out_shape=[
            jax.ShapeDtypeStruct((chips, 2, half // chips, cols), jnp.float32),
            jax.ShapeDtypeStruct((2, rows, cols), jnp.bfloat16),
        ],
        cost_estimate=cost(half * cols, 12, 24),
    )(place, own, mate, phase)


def beside(tiles, step):
    lane = lax.broadcasted_iota(jnp.int32, tiles[0].shape, 1)
    turned = [pltpu.roll(tile, (-step) % LANES, 1) for tile in tiles]
    count = len(tiles)
    out = []
    for c in range(count):
        if step > 0:
            other = turned[c + 1] if c + 1 < count else jnp.zeros_like(tiles[0])
            out.append(jnp.where(lane >= LANES - step, other, turned[c]))
        else:
            other = turned[c - 1] if c > 0 else jnp.zeros_like(tiles[0])
            out.append(jnp.where(lane < -step, other, turned[c]))
    return out


def put_column_sums(field_ref, sums_ref):
    cols, rows = sums_ref.shape[1], sums_ref.shape[2] // 2
    for c in range(0, cols, CHUNK):
        total = field_ref[PAD + c : PAD + c + CHUNK]
        for j in (1, 2, 3):
            total = total + (field_ref[PAD + c + j : PAD + c + j + CHUNK] + field_ref[PAD + c - j : PAD + c - j + CHUNK])
            high = total.astype(jnp.bfloat16)
            sums_ref[j - 1, c : c + CHUNK, :rows] = high
            sums_ref[j - 1, c : c + CHUNK, rows:] = (total - high.astype(jnp.float32)).astype(jnp.bfloat16)


def looked(sums_ref, band_ref, half, columns):
    box = [
        lax.dot_general(band_ref[h], sums_ref[h, columns, :], (((1,), (1,)), ((), ())), preferred_element_type=jnp.float32)
        for h in range(3)
    ]
    return jnp.where(half == 1, box[0], jnp.where(half == 2, box[1], box[2]))


def main_kernel(
    dates_dev, slot_ref, valid_ref, place_ref, slc_ref, mine_ref, other_half_ref, half_ref, band_ref,
    filtered_ref, gamma_ref, flat_ref, weight_ref, inverse_ref, field_ref, sums_ref, unit_ref,
):
    cols, rows = weight_ref.shape
    tiles = cols // LANES
    wide = 2 * LANES
    step = pl.program_id(0)
    date = step // REACH
    far = date + step % REACH + 1

    def tile_of(c):
        return slice(c * LANES, (c + 1) * LANES)

    @pl.when(step == 0)
    def _():
        unit_ref[:, :, 0:PAD, :] = jnp.zeros((2, tiles, PAD, LANES), jnp.float32)
        unit_ref[:, :, rows + PAD : rows + 2 * PAD, :] = jnp.zeros((2, tiles, PAD, LANES), jnp.float32)
        field_ref[:, 0:PAD, :] = jnp.zeros((2, PAD, rows), jnp.float32)
        field_ref[:, cols + PAD : cols + 2 * PAD, :] = jnp.zeros((2, PAD, rows), jnp.float32)
        part = rows // 2
        start = pl.multiple_of(place_ref[0] * part, part)
        flat_ref[pl.ds(start, part), :] = mine_ref[...]
        flat_ref[pl.ds(pl.multiple_of(part - start, part), part), :] = other_half_ref[...]
        for c in range(tiles):
            weight_ref[tile_of(c)] = flat_ref[:, tile_of(c)].T

        def power_date(d, carry):
            for c in range(tiles):
                real, imag = slc_ref[d, 0, tile_of(c)], slc_ref[d, 1, tile_of(c)]
                field_ref[0, PAD + c * LANES : PAD + (c + 1) * LANES] = weight_ref[tile_of(c)] * (real * real + imag * imag)
            put_column_sums(field_ref.at[0], sums_ref.at[0])
            valid = valid_ref[d] != 0
            for n in range(0, cols, wide):
                columns = slice(n, n + wide)
                power = looked(sums_ref.at[0], band_ref, half_ref[:, columns], columns)
                inverse_ref[d, :, columns] = jnp.where(valid, lax.rsqrt(power), 0.0)
            return carry

        lax.fori_loop(0, dates_dev + REACH, power_date, 0)

    for c in range(0, cols, 4 * CHUNK):
        here = slice(c, c + 4 * CHUNK)
        weight = weight_ref[here]
        real, imag = weight * slc_ref[date, 0, here], weight * slc_ref[date, 1, here]
        far_real, far_imag = slc_ref[far, 0, here], slc_ref[far, 1, here]
        there = slice(PAD + c, PAD + c + 4 * CHUNK)
        field_ref[0, there] = real * far_real + imag * far_imag
        field_ref[1, there] = imag * far_real - real * far_imag
    for part in range(2):
        put_column_sums(field_ref.at[part], sums_ref.at[part])

    for n in range(0, cols, wide):
        columns = slice(n, n + wide)
        half = half_ref[:, columns]
        scale = inverse_ref[date, :, columns] * inverse_ref[far, :, columns]
        for part in range(2):
            unit = looked(sums_ref.at[part], band_ref, half, columns) * scale
            for k in range(wide // LANES):
                unit_ref[part, n // LANES + k, PAD : rows + PAD, :] = unit[:, tile_of(k)]

    for row in range(0, rows, CHUNK):
        units, means = [], []
        for part in range(2):
            centre = [unit_ref[part, c, row + PAD : row + PAD + CHUNK, :] for c in range(tiles)]
            column = [
                centre[c]
                + unit_ref[part, c, row + PAD - 1 : row + PAD - 1 + CHUNK, :]
                + unit_ref[part, c, row + PAD + 1 : row + PAD + 1 + CHUNK, :]
                for c in range(tiles)
            ]
            after, before = beside(column, 1), beside(column, -1)
            units.append(centre)
            means.append([(m + a + b) * (1.0 / 9.0) for m, a, b in zip(column, after, before)])
        for c in range(tiles):
            real, imag = units[0][c], units[1][c]
            gamma = jnp.sqrt(real * real + imag * imag)
            for part in range(2):
                mean = means[part][c]
                value = mean + gamma * (units[part][c] - mean)
                filtered_ref[0, 0, part, row : row + CHUNK, tile_of(c)] = value.astype(jnp.bfloat16)
            gamma_ref[0, 0, row : row + CHUNK, tile_of(c)] = gamma.astype(jnp.bfloat16)


def band_of(rows):
    gap = np.abs(np.arange(rows)[:, None] - np.arange(rows)[None, :])
    band = np.stack([(gap <= h).astype(np.float32) for h in (1, 2, 3)])
    return jnp.asarray(np.concatenate([band, band], axis=2), jnp.bfloat16)


def interferograms(place, slc, weights, look_half, slot, valid):
    ext, _, cols, rows = slc.shape
    dates_dev = ext - REACH
    whole = pl.BlockSpec(memory_space=pltpu.VMEM)
    spec = pltpu.PrefetchScalarGridSpec(
        num_scalar_prefetch=3,
        grid=(dates_dev * REACH,),
        in_specs=[whole] * 5,
        out_specs=[
            pl.BlockSpec((1, 1, 2, rows, cols), lambda s, slot, valid, place: (s // REACH, slot[s], 0, 0, 0)),
            pl.BlockSpec((1, 1, rows, cols), lambda s, slot, valid, place: (s // REACH, slot[s], 0, 0)),
        ],
        scratch_shapes=[
            pltpu.VMEM((rows, cols), jnp.float32),
            pltpu.VMEM((cols, rows), jnp.float32),
            pltpu.VMEM((ext, rows, cols), jnp.float32),
            pltpu.VMEM((2, cols + 2 * PAD, rows), jnp.float32),
            pltpu.VMEM((2, 3, cols, 2 * rows), jnp.bfloat16),
            pltpu.VMEM((2, cols // LANES, rows + 2 * PAD, LANES), jnp.float32),
        ],
    )
    return pl.pallas_call(
        functools.partial(main_kernel, dates_dev),
        grid_spec=spec,
        out_shape=[
            jax.ShapeDtypeStruct((dates_dev, REACH, 2, rows, cols), jnp.bfloat16),
            jax.ShapeDtypeStruct((dates_dev, REACH, rows, cols), jnp.bfloat16),
        ],
        compiler_params=pltpu.CompilerParams(vmem_limit_bytes=24 * 2**20),
        cost_estimate=pl.CostEstimate(flops=10**10, bytes_accessed=2 * 10**7, transcendentals=10**6),
    )(slot, valid, place, slc, *weights, look_half, band_of(rows))


def send(value, pairs):
    return lax.ppermute(value, "date", pairs)


def spread_weight(first, second, total_dates):
    return 1.0 / (1.0 + DISP_GAIN * (total_dates * second / (first * first) - 1.0))


def local(amplitude, phase, offset_code, look_half):
    dates_dev, rows, cols = amplitude.shape
    count = lax.axis_size("date")
    chips = count // 2
    total_dates = dates_dev * count
    index = lax.axis_index("date")
    place = jnp.stack([index % 2, index // 2]).astype(jnp.int32)
    mate_pairs = [(i, i ^ 1) for i in range(count)]
    to_even = [(i, i - 1) for i in range(1, count, 2)]
    next_pairs = [(i, i - 2) for i in range(2, count)]
    last_pairs = [(i, i - 3) for i in range(4, count, 2)]
    groups = [[core + 2 * chip for chip in range(chips)] for core in range(2)]

    amp_mate = send(amplitude, mate_pairs)
    pieces, early = moment_pieces(place, amplitude, amp_mate, phase, chips)
    moments = jnp.sum(lax.all_to_all(pieces, "date", 0, 0, axis_index_groups=groups), axis=0)
    following = [send(amplitude, next_pairs)]
    last = send(early, last_pairs)
    phase_mate = send(phase, to_even)
    weight = spread_weight(moments[0], moments[1], total_dates)
    copies = jnp.broadcast_to(weight[None], (chips,) + weight.shape)
    mine = lax.all_to_all(copies, "date", 0, 0, axis_index_groups=groups).reshape(rows // 2, cols)
    (late,) = after([phase], copies)
    following = [*after(following, copies), send(late, next_pairs)]
    via = [send(x, mate_pairs) for x in following]
    weights = (mine, send(mine, mate_pairs))
    near = slc_turned(first_slc_kernel, *following)
    slc = slc_turned(second_slc_kernel, amp_mate, phase_mate, *via, last, amplitude, phase, begun=near)
    valid = (index * dates_dev + jnp.arange(dates_dev + REACH) < total_dates).astype(jnp.int32)
    same = offset_code[:, None, :] == jnp.arange(REACH, dtype=jnp.int32)[None, :, None]
    slot = jnp.sum(jnp.where(same, jnp.arange(REACH, dtype=jnp.int32), 0), axis=2, dtype=jnp.int32).reshape(-1)
    filtered, coherence = interferograms(place, slc, weights, look_half, slot, valid)
    return filtered, coherence


def solution(mesh):
    return jax.shard_map(
        local,
        mesh=mesh,
        in_specs=(P("date", "grp", None), P("date", "grp", None), P("date", None), P("grp", None)),
        out_specs=(P("date", None, None, "grp", None), P("date", None, "grp", None)),
        check_vma=False,
    )
```
